256 devices in a mesh: row: 32 (over z, x), col: 8 (over y, core).
Axes of the slice: x: 4, y: 4, z: 8, core: 2. Of those that a mesh axis runs over, the one named last changes fastest.
Arguments:
- momentum: bfloat16 [16384, 16384], P('row', 'col'), may hold values from -16 to 16
- gradient: bfloat16 [16384, 16384], P('row', 'col'), may hold values from -6 to 6
- right_basis: bfloat16 [1024, 16384], P('row', 'col'), may hold values from -1 to 1
Outputs:
- momentum_next: bfloat16 [16384, 16384], P('row', 'col')
- basis_next: float32 [1024, 16384], P('row', 'col')
- update: bfloat16 [16384, 16384], P('row', 'col')
The draws below stay inside these ranges and needn't reach their ends.
All inputs are finite; a program needn't handle non-finite values.
Results may differ from the reference program's by a relative error of at most 0.02.
Values may be sent and summed in bfloat16 or wider, within the bound.
No kernel may reach another device: no remote copies, remote signals or barrier semaphores. Data moves between devices by JAX's collectives and lax.ppermute only.
A program may use at most 128 MiB of HBM per device.

```python
import math
import jax
import jax.numpy as jnp
from jax import lax

D = 16384
RANK = 1024


def shared_directions(key):
    values = jax.random.normal(jax.random.fold_in(key, 11), (RANK, D), jnp.float32)
    return jnp.clip(values, -6.0, 6.0) * D ** (-0.5)


def draw_right_basis(key, part):
    return shared_directions(key).astype(jnp.bfloat16)


def draw_momentum(key, part):
    directions = shared_directions(key)
    highest = 4.0
    column_low = 0.6
    column_high = 1.8
    residue = jnp.clip(jax.random.normal(jax.random.fold_in(key, 37), (D, D), jnp.float32), -6.0, 6.0)
    scales = jnp.exp(jax.random.uniform(jax.random.fold_in(key, 41), (RANK,), jnp.float32, minval=0.0, maxval=math.log(highest)))
    coefficients = jax.random.normal(jax.random.fold_in(key, 23), (D, RANK), jnp.float32)
    coefficients = jnp.clip(coefficients, -6.0, 6.0) * scales[None, :] * math.sqrt(D / RANK)
    in_span = jnp.dot(coefficients, directions)
    position = jnp.arange(D, dtype=jnp.float32) / float(D - 1)
    column_scale = column_low * jnp.exp(position * math.log(column_high / column_low))
    return jnp.clip((in_span + residue) * column_scale[None, :], -16.0, 16.0).astype(jnp.bfloat16)


def level_of(own_key, extent, cuts, smallest, high):
    def one(axis_at, blocks):
        draws = jax.random.uniform(jax.random.fold_in(jax.random.fold_in(own_key, 6), axis_at), (blocks,), jnp.float32, smallest / len(cuts), high / len(cuts))
        return jnp.repeat(jnp.exp(draws), extent[axis_at] // blocks).reshape((-1,) + (1,) * (len(extent) - axis_at - 1))

    factor_of = one(*cuts[0])
    for cut in cuts[1:]:
        factor_of = factor_of * one(*cut)
    return factor_of


def centred(stream_key, shape, spread, limit, shards=(), kind=jnp.bfloat16):
    result = jax.random.normal(stream_key, shape, jnp.float32) * spread
    if len(shards) > 0:
        result = level_of(stream_key, shape, shards, -0.22, 0.18) * result
    return jnp.clip(result, min=-limit, max=limit).astype(kind)


def setup_inputs(seed: int = 0) -> dict:
    arg_keys = jax.random.split(jax.random.key(seed), 4)
    return {
        "momentum": draw_momentum(jax.random.fold_in(arg_keys[3], 71), 0),
        "gradient": centred(arg_keys[1], (D, D), 1.0, 6.0, ((0, 32), (1, 8))),
        "right_basis": draw_right_basis(jax.random.fold_in(arg_keys[3], 71), 0),
    }


momentum_decay = 0.95
epsilon = 1e-06

def reference(momentum, gradient, right_basis):
    buffer = (momentum.astype(jnp.float32) + gradient.astype(jnp.float32)).astype(jnp.bfloat16)
    projected = jnp.dot(buffer.astype(jnp.float32), right_basis.T.astype(jnp.float32), preferred_element_type=jnp.float32)
    gram_matrix = jnp.dot(projected.T, projected, precision=lax.Precision.HIGHEST)
    lower_factor = jnp.linalg.cholesky(gram_matrix)
    orthonormal = jax.scipy.linalg.solve_triangular(lower_factor, projected.T, lower=True).T.astype(jnp.bfloat16)
    right_new = jnp.dot(orthonormal.T.astype(jnp.float32), buffer.astype(jnp.float32), preferred_element_type=jnp.float32).astype(jnp.bfloat16)
    right_wide = right_new.astype(jnp.float32)
    inverse_norm = lax.rsqrt(lax.optimization_barrier(jnp.sum(right_wide * right_wide, axis=1, keepdims=True)) + epsilon)
    basis_next = right_wide * inverse_norm
    basis_low = basis_next.astype(jnp.bfloat16)
    feedback = jnp.dot(orthonormal.astype(jnp.float32), right_new.astype(jnp.float32), preferred_element_type=jnp.float32)
    momentum_next = (buffer.astype(jnp.float32) - (1.0 - momentum_decay) * feedback).astype(jnp.bfloat16)
    update_scale = D / math.sqrt(RANK)
    update = (update_scale * jnp.dot(orthonormal.astype(jnp.float32), basis_low.astype(jnp.float32), preferred_element_type=jnp.float32)).astype(jnp.bfloat16)
    return (momentum_next, basis_next, update)
```

```python
import math

import jax
import jax.numpy as jnp
from jax import lax
from jax.experimental import pallas as pl
from jax.experimental.pallas import tpu as pltpu
from jax.sharding import Mesh
from jax.sharding import PartitionSpec as P

D = 16384
RANK = 1024
BLOCK = 128
ROW = ("z", "x")
COL = ("y", "core")
f32 = jnp.float32
bf16 = jnp.bfloat16


momentum_decay = 0.95
epsilon = 1e-06


def halves(value):
    high = value.astype(bf16)
    return high, (value - high.astype(f32)).astype(bf16)


def product(left, right, dims):
    high, low = left
    upper, lower = right

    def one(a, b):
        return lax.dot_general(a, b, (dims, ((), ())), preferred_element_type=f32)

    return one(high, upper) + (one(high, lower) + one(low, upper))


def reciprocal(value):
    guess = pl.reciprocal(value, approx=True)
    guess = guess * (2.0 - value * guess)
    return guess * (2.0 - value * guess)


def inverse_root(value):
    guess = lax.rsqrt(value)
    for _ in range(2):
        guess = guess * (1.5 - 0.5 * value * guess * guess)
    return guess


def spread_row(tile, row):
    return jnp.broadcast_to(tile[row : row + 1, :], tile.shape)


def spread_lane(tile, lane):
    return jnp.broadcast_to(tile[:, lane : lane + 1], tile.shape)


def block_inverse(tiles):
    count = len(tiles)
    lane = lax.broadcasted_iota(jnp.int32, (8, BLOCK), 1)
    sub = lax.broadcasted_iota(jnp.int32, (8, BLOCK), 0)
    tiles = list(tiles)
    done = []
    for step in range(count):
        base = 8 * step
        inside = (lane >= base) & (lane < base + 8)
        columns = [spread_lane(tiles[step], base + j) for j in range(8)]
        whole_columns = list(columns)
        partial = jnp.where(inside, jnp.where(lane - base == sub, 1.0, 0.0), tiles[step])
        whole = partial
        pivots = jnp.zeros((8, BLOCK), f32)
        for j in range(8):
            own = sub == j
            pivot = spread_row(columns[j], j)
            inverse = reciprocal(pivot)
            pivots = jnp.where(own, pivot, pivots)
            below = jnp.where(sub > j, columns[j], 0.0) * inverse
            others = jnp.where(own, 0.0, whole_columns[j]) * inverse
            partial = partial - below * spread_row(partial, j)
            row = spread_row(whole, j)
            whole = jnp.where(own, row * inverse, whole - others * row)
            for later in range(j + 1, 8):
                row = spread_row(whole_columns[later], j)
                columns[later] = columns[later] - below * spread_row(columns[later], j)
                whole_columns[later] = jnp.where(
                    own, row * inverse, whole_columns[later] - others * row
                )
        done.append(partial * inverse_root(pivots))
        rows = [spread_row(whole, j) for j in range(8)]
        for later in range(step + 1, count):
            tile = tiles[later]
            terms = [spread_lane(tile, base + j) * rows[j] for j in range(8)]
            while len(terms) > 1:
                terms = [a + b for a, b in zip(terms[::2], terms[1::2])]
            tiles[later] = jnp.where(inside, 0.0, tile) - terms[0]
    return [jnp.where(lane <= sub + 8 * step, done[step], 0.0) for step in range(count)]


def factor_kernel(gram_ref, high_ref, low_ref, work_ref):
    blocks = RANK // BLOCK
    for i in range(blocks):
        for j in range(i, blocks):
            if j - i <= blocks // 2:
                source, place = i, j - i
            else:
                source, place = j, blocks - (j - i)
            work_ref[i * BLOCK : (i + 1) * BLOCK, j * BLOCK : (j + 1) * BLOCK] = gram_ref[
                source, place * BLOCK : (place + 1) * BLOCK, :
            ]
    for step in range(blocks):
        a = step * BLOCK
        b = a + BLOCK
        tiles = [work_ref[a + 8 * i : a + 8 * i + 8, a:b] for i in range(BLOCK // 8)]
        inverse = jnp.concatenate(block_inverse(tiles), axis=0)
        inverse_pair = halves(inverse)
        parts = []
        row = product(inverse_pair, halves(work_ref[a:b, :]), ((1,), (0,)))
        if step:
            parts.append(row[:, :a])
        parts.append(inverse)
        if b < RANK:
            parts.append(row[:, b:])
        row = halves(jnp.concatenate(parts, axis=1))
        for out, value in zip((high_ref, low_ref), row):
            out[a:b, :b] = value[:, :b]
            if b < RANK:
                out[a:b, b:] = jnp.zeros((BLOCK, RANK - b), bf16)
        for c in range(b, RANK, BLOCK):
            d = c + BLOCK
            factor = tuple(value[:, c:d] for value in row)
            left = product(factor, tuple(value[:, :b] for value in row), ((0,), (0,)))
            if step:
                work_ref[c:d, :a] = work_ref[c:d, :a] - left[:, :a]
            work_ref[c:d, a:b] = -left[:, a:]
            right = product(factor, tuple(value[:, c:] for value in row), ((0,), (0,)))
            work_ref[c:d, c:] = work_ref[c:d, c:] - right


def factor_inverse(gram_blocks):
    out = jax.ShapeDtypeStruct((RANK, RANK), bf16)
    return pl.pallas_call(
        factor_kernel,
        out_shape=(out, out),
        in_specs=[pl.BlockSpec(memory_space=pltpu.VMEM)],
        out_specs=(pl.BlockSpec(memory_space=pltpu.VMEM),) * 2,
        scratch_shapes=[pltpu.VMEM((RANK, RANK), f32)],
        compiler_params=pltpu.CompilerParams(vmem_limit_bytes=40 * 1024 * 1024),
        name="factor_inverse",
    )(gram_blocks)


def shifted(value, axis, step):
    size = lax.axis_size(axis)
    return lax.ppermute(value, axis, [(i, (i + step) % size) for i in range(size)])


def steps_of(size):
    order = []
    for distance in range(1, size // 2 + 1):
        for step in (distance, size - distance):
            if step not in order:
                order.append(step)
    return order


def gather_direct(value, axis):
    size = lax.axis_size(axis)
    me = lax.axis_index(axis)
    out = jnp.zeros((size, *value.shape), value.dtype)
    out = lax.dynamic_update_index_in_dim(out, value, me, 0)
    for step in steps_of(size):
        got = shifted(value, axis, step)
        out = lax.dynamic_update_index_in_dim(out, got, (me - step) % size, 0)
    return out


def gather_ring(value, axis):
    size = lax.axis_size(axis)
    me = lax.axis_index(axis)
    out = jnp.zeros((size, *value.shape), value.dtype)
    out = lax.dynamic_update_index_in_dim(out, value, me, 0)
    up = down = value
    for step in range(1, size // 2 + 1):
        up = shifted(up, axis, 1)
        out = lax.dynamic_update_index_in_dim(out, up, (me - step) % size, 0)
        if 2 * step < size:
            down = shifted(down, axis, size - 1)
            out = lax.dynamic_update_index_in_dim(out, down, (me + step) % size, 0)
    return out


def scatter_sum_direct(value, axis, sent=None):
    size = lax.axis_size(axis)
    me = lax.axis_index(axis)
    total = lax.dynamic_index_in_dim(value, me, 0, keepdims=False).astype(f32)
    outgoing = value if sent is None else value.astype(sent)
    for step in steps_of(size):
        part = lax.dynamic_index_in_dim(outgoing, (me + step) % size, 0, keepdims=False)
        total = total + shifted(part, axis, step).astype(f32)
    return total


def gathered_basis(shard):
    ranks, width = shard.shape
    cut = width // 2
    first = gather_direct(shard[:, :cut], "z")
    first = gather_direct(first, "x")
    first = first.transpose(1, 0, 2, 3).reshape(RANK, cut)
    second = gather_direct(shard[:, cut:], "x")
    second = gather_ring(second, "z").reshape(RANK, width - cut)
    return first, second


def summed_projection(partial):
    rows = partial.shape[0]
    half = scatter_sum_direct(partial.reshape(2, rows // 2, RANK), "core", bf16)
    own = scatter_sum_direct(half.reshape(4, rows // 8, RANK), "y", bf16).astype(bf16)
    half = gather_direct(own, "y").reshape(rows // 2, RANK)
    return gather_direct(half, "core").reshape(rows, RANK)


def gram_blocks_of(projected):
    blocks = RANK // BLOCK
    me = lax.axis_index(COL)
    parts = []
    for distance in range(blocks // 2 + 1):
        other = (me + distance) % blocks
        low, high = jnp.minimum(me, other), jnp.maximum(me, other)
        left = lax.dynamic_slice_in_dim(projected, low * BLOCK, BLOCK, 1)
        right = lax.dynamic_slice_in_dim(projected, high * BLOCK, BLOCK, 1)
        parts.append(
            lax.dot_general(left, right, (((0,), (0,)), ((), ())), preferred_element_type=f32)
        )
    return jnp.concatenate(parts, axis=0)


def summed_gram(partial):
    lines = partial.shape[0]
    total = scatter_sum_direct(partial.reshape(4, lines // 4, BLOCK), "x")
    total = scatter_sum_direct(total.reshape(8, lines // 32, BLOCK), "z")
    total = gather_direct(total, "z").reshape(lines // 4, BLOCK)
    total = gather_direct(total, "y")
    total = gather_direct(total, "x")
    total = gather_direct(total, "core")
    return total.transpose(2, 0, 1, 3, 4).reshape(8, lines, BLOCK)


def summed_right(partial):
    own = lax.psum_scatter(partial.astype(bf16), "z", scatter_dimension=0, tiled=True)
    lines, width = own.shape
    own = scatter_sum_direct(own.reshape(4, lines // 4, width), "x").astype(bf16)
    own = gather_direct(own, "x").reshape(lines, width)
    return lax.all_gather(own, "z", axis=0, tiled=True)


def total_by_col(values):
    total = values
    for step in steps_of(8):
        total = total + shifted(values, COL, step)
    return total


def contract(left, right, dims):
    return lax.dot_general(left, right, (dims, ((), ())), preferred_element_type=f32)


def body(momentum, gradient, right_basis):
    buffer = (momentum.astype(f32) + gradient.astype(f32)).astype(bf16)
    rank_rows = right_basis.shape[0]
    first, second = gathered_basis(right_basis)
    cut = first.shape[1]
    partial = contract(buffer[:, :cut], first, ((1,), (1,))) + contract(
        buffer[:, cut:], second, ((1,), (1,))
    )
    projected = summed_projection(partial)
    gram_blocks = summed_gram(gram_blocks_of(projected))
    crossed = summed_right(contract(projected, buffer, ((0,), (0,))))
    high, low = factor_inverse(gram_blocks)
    right_new = (
        contract(high, crossed, ((1,), (0,))) + contract(low, crossed, ((1,), (0,)))
    ).astype(bf16)
    orthonormal = (
        contract(projected, high, ((1,), (1,))) + contract(projected, low, ((1,), (1,)))
    ).astype(bf16)
    right_wide = right_new.astype(f32)
    inverse_norm = lax.rsqrt(total_by_col(jnp.sum(right_wide * right_wide, axis=1)) + epsilon)
    feedback = contract(orthonormal, right_new, ((1,), (0,)))
    momentum_next = (buffer.astype(f32) - (1.0 - momentum_decay) * feedback).astype(bf16)
    scaled = (orthonormal.astype(f32) * inverse_norm[None, :]).astype(bf16)
    update_scale = D / math.sqrt(RANK)
    update = (update_scale * contract(scaled, right_new, ((1,), (0,)))).astype(bf16)
    offset = lax.axis_index(ROW) * rank_rows
    own = lax.dynamic_slice_in_dim(right_new, offset, rank_rows, 0).astype(f32)
    basis_next = own * lax.dynamic_slice_in_dim(inverse_norm, offset, rank_rows, 0)[:, None]
    return (momentum_next, basis_next, update)


def solution(mesh):
    finer = Mesh(mesh.devices.reshape(8, 4, 4, 2), ("z", "x", "y", "core"))
    return jax.shard_map(
        body,
        mesh=finer,
        in_specs=(P(ROW, COL), P(ROW, COL), P(ROW, COL)),
        out_specs=(P(ROW, COL), P(ROW, COL), P(ROW, COL)),
        check_vma=False,
    )
```
